512 devices in a mesh: lon: 32 (over y_hi, x, core), lat: 16 (over y_lo, z).
Axes of the slice: x: 4, y: 8 (y_hi: 4, y_lo: 2; y = y_hi * 2 + y_lo), z: 8, core: 2. Of those that a mesh axis runs over, the one named last changes fastest.
Arguments:
- tokens: bfloat16 [4, 192, 384, 512], P(None, 'lat', 'lon'), may hold values from -6 to 6
- w_qkv: bfloat16 [512, 1536], P('lat', 'lon'), may hold values from -1 to 1
- w_proj: bfloat16 [512, 512], P('lat', 'lon'), may hold values from -0.25 to 0.25
- w_up: bfloat16 [512, 2048], P('lat', 'lon'), may hold values from -0.25 to 0.25
- w_down: bfloat16 [2048, 512], P('lat', 'lon'), may hold values from -0.125 to 0.125
Outputs:
- result: bfloat16 [4, 192, 384, 512], P(None, 'lat', 'lon')
The draws below stay inside these ranges and needn't reach their ends.
All inputs are finite; a program needn't handle non-finite values.
Results may differ from the reference program's by a relative error of at most 0.011.
Values may be sent and summed in bfloat16 or wider, within the bound.
No kernel may reach another device: no remote copies, remote signals or barrier semaphores. Data moves between devices by JAX's collectives and lax.ppermute only.
A program may use at most 64 MiB of HBM per device.

```python
import jax
import jax.numpy as jnp
from jax import lax

D = 512
FF = 2048
HD = 64
HEADS = 8
LEV = 4
WZ = 2
WH = 6
WW = 12
NLAT = 192
NLON = 384


def draw_w_qkv(key, part):
    key = jax.random.fold_in(key, 11)
    first = jax.random.fold_in(key, 0)
    base = jax.random.normal(first, (D, 3 * D), jnp.float32) * D ** (-0.5)
    result = base
    return jnp.clip(result, -1.0, 1.0).astype(jnp.bfloat16)


def shard_levels(stream_key, extent, cuts, least, top_value):
    def one(position, blocks):
        heights = jax.random.uniform(jax.random.fold_in(jax.random.fold_in(stream_key, 6), position), (blocks,), jnp.float32, least / len(cuts), top_value / len(cuts))
        return jnp.repeat(jnp.exp(heights), extent[position] // blocks).reshape((-1,) + (1,) * (len(extent) - position - 1))

    factor_of = one(*cuts[0])
    for cut in cuts[1:]:
        factor_of = factor_of * one(*cut)
    return factor_of


def scatter_about(key, dims, deviation, bound, shards=(), kind=jnp.bfloat16):
    values = jax.random.normal(key, dims, jnp.float32) * deviation
    if len(shards) > 0:
        values = shard_levels(key, dims, shards, -0.22, 0.18) * values
    return jnp.clip(values, min=-bound, max=bound).astype(kind)


def setup_inputs(seed: int = 0) -> dict:
    key_of = jax.random.split(jax.random.key(seed), 6)
    return {
        "tokens": scatter_about(key_of[0], (LEV, NLAT, NLON, D), 1.0, 6.0, ((1, 16), (2, 32))),
        "w_qkv": draw_w_qkv(jax.random.fold_in(key_of[5], 71), 0),
        "w_proj": scatter_about(key_of[2], (D, D), D ** -0.5, 0.25, ((0, 16), (1, 32))),
        "w_up": scatter_about(key_of[3], (D, FF), D ** -0.5, 0.25, ((0, 16), (1, 32))),
        "w_down": scatter_about(key_of[4], (FF, D), FF ** -0.5, 0.125, ((0, 16), (1, 32))),
    }


EPS = 1e-05

def layer_norm(values):
    wide = values.astype(jnp.float32)
    center = lax.optimization_barrier(jnp.mean(wide, axis=-1, keepdims=True))
    spread = lax.optimization_barrier(jnp.mean((wide - center) ** 2, axis=-1, keepdims=True))
    return ((wide - center) * lax.rsqrt(spread + EPS)).astype(jnp.bfloat16)

def region(positions, total, window):
    return jnp.where(positions < total - window, 0, jnp.where(positions < total - window // 2, 1, 2)).astype(jnp.int32)

def to_windows(grid):
    levels, lat_rows, lon_cols, channels = grid.shape
    shaped = grid.reshape(levels // WZ, WZ, lat_rows // WH, WH, lon_cols // WW, WW, channels)
    shaped = shaped.transpose(0, 2, 4, 1, 3, 5, 6)
    return shaped.reshape(-1, WZ * WH * WW, channels)

def from_windows(windows, levels, lat_rows, lon_cols):
    channels = windows.shape[-1]
    shaped = windows.reshape(levels // WZ, lat_rows // WH, lon_cols // WW, WZ, WH, WW, channels)
    shaped = shaped.transpose(0, 3, 1, 4, 2, 5, 6)
    return shaped.reshape(levels, lat_rows, lon_cols, channels)

def attend(windows_qkv, window_labels):
    count, span, triple = windows_qkv.shape
    split = windows_qkv.reshape(count, span, 3, HEADS, HD).astype(jnp.float32)
    scores = jnp.einsum('wqhd,wkhd->whqk', split[:, :, 0], split[:, :, 1]) * HD ** (-0.5)
    allowed = window_labels[:, None, :, None] == window_labels[:, None, None, :]
    scores = jnp.where(allowed, scores, -1000000000.0)
    probabilities = jax.nn.softmax(scores, axis=-1).astype(jnp.bfloat16)
    mixed = jnp.einsum('whqk,wkhd->wqhd', probabilities.astype(jnp.float32), split[:, :, 2])
    return mixed.astype(jnp.bfloat16).reshape(count, span, D)

def reference(tokens, w_qkv, w_proj, w_up, w_down):
    rolled = jnp.roll(tokens, (-(WZ // 2), -(WH // 2), -(WW // 2)), axis=(0, 1, 2))
    level_labels = region(jnp.arange(LEV), LEV, WZ)

    def band(band_index):
        grid = lax.dynamic_slice_in_dim(rolled, band_index * WH, WH, 1)
        lat_positions = band_index * WH + jnp.arange(WH)
        labels = level_labels[:, None] * 3 + region(lat_positions, NLAT, WH)[None, :]
        labels = jnp.broadcast_to(labels[:, :, None, None], (LEV, WH, NLON, 1))
        window_labels = to_windows(labels)[:, :, 0]
        flat = grid.reshape(-1, D)
        normed = layer_norm(flat)
        qkv_rows = jnp.dot(normed, w_qkv, preferred_element_type=jnp.float32).astype(jnp.bfloat16)
        windows = to_windows(qkv_rows.reshape(LEV, WH, NLON, 3 * D))
        mixed = from_windows(attend(windows, window_labels), LEV, WH, NLON).reshape(-1, D)
        attended = (flat.astype(jnp.float32) + jnp.dot(mixed, w_proj, preferred_element_type=jnp.float32)).astype(jnp.bfloat16)
        hidden = jnp.dot(layer_norm(attended), w_up, preferred_element_type=jnp.float32)
        expanded = jax.nn.gelu(hidden, approximate=False).astype(jnp.bfloat16)
        block = attended.astype(jnp.float32) + jnp.dot(expanded, w_down, preferred_element_type=jnp.float32)
        return block.astype(jnp.bfloat16).reshape(LEV, WH, NLON, D)
    bands = lax.map(band, jnp.arange(NLAT // WH))
    block = bands.transpose(1, 0, 2, 3, 4).reshape(LEV, NLAT, NLON, D)
    return jnp.roll(block, (WZ // 2, WH // 2, WW // 2), axis=(0, 1, 2))
```

```python
import functools

import jax
import jax.numpy as jnp
from jax import lax
from jax.experimental import pallas as pl
from jax.experimental.pallas import tpu as pltpu
from jax.sharding import PartitionSpec as P

D = 512
FF = 2048
HD = 64
HEADS = 8
WH = 6
EPS = 1e-05
F32 = jnp.float32
BF16 = jnp.bfloat16

NZ, NX, NYH = 8, 4, 4
LAT, LON = 16, 32
VMEM_LIMIT = 56 * 1024 * 1024


def lat_parts(i):
    return i // NZ, i % NZ


def lon_parts(j):
    return j // (2 * NX), (j // 2) % NX, j % 2


def class_of(i, j):
    return (lon_parts(j)[1] + 2 * lat_parts(i)[0]) % 4


def grouped(size, key):
    found = {}
    for index in range(size):
        found.setdefault(key(index), []).append(index)
    return list(found.values())


CLASS_GROUPS = grouped(
    LAT * LON,
    lambda n: (class_of(n // LON, n % LON), lon_parts(n % LON)[0], n % 2),
)
Y_GROUPS = grouped(LON, lambda j: lon_parts(j)[1:])


def dot_nt(a, b):
    return lax.dot_general(a, b, (((1,), (1,)), ((), ())), preferred_element_type=F32)


def kernel_call(body, out_shape, scratch=(), smem=0, operands=0, cost=None):
    vmem = pl.BlockSpec(memory_space=pltpu.VMEM)
    in_specs = [pl.BlockSpec(memory_space=pltpu.SMEM)] * smem + [vmem] * operands
    outs = jax.tree.map(lambda _: vmem, out_shape)
    return pl.pallas_call(
        body,
        out_shape=out_shape,
        in_specs=in_specs,
        out_specs=outs,
        scratch_shapes=list(scratch),
        compiler_params=pltpu.CompilerParams(vmem_limit_bytes=VMEM_LIMIT),
        cost_estimate=cost,
    )


def pack_kernel(qkv_ref, proj_ref, up_ref, down_ref, out_ref):
    rows = jnp.concatenate(
        [qkv_ref[...].astype(F32), proj_ref[...].astype(F32), up_ref[...].astype(F32)], axis=1
    )
    blob = jnp.concatenate([rows, down_ref[...].astype(F32).T], axis=0).astype(BF16)
    out_ref[...] = jnp.broadcast_to(blob[None], out_ref.shape)


def unit_kernel(in_ref, out_ref):
    for half in range(2):
        for z in range(NZ):
            block = in_ref[half * NZ + z]
            out_ref[half, 128 + 16 * (z // 2) : 144 + 16 * (z // 2), 128 * (z % 2) : 128 * (z % 2) + 128] = block[32:48]
        for quad in range(2):
            first = half * NZ + 4 * quad
            rows = jnp.concatenate([in_ref[first + t, 0:32, :] for t in range(4)], axis=0)
            out_ref[half, 0:128, 128 * quad : 128 * quad + 128] = rows.astype(F32).T.astype(BF16)


def half_kernel(s_ref, own_ref, one_ref, two_ref, three_ref, qp_ref, up_ref, down_ref):
    mine = s_ref[0]
    for offset, ref in enumerate((own_ref, one_ref, two_ref, three_ref)):
        for y_hi in range(NYH):
            for y_lo in range(2):
                x = lax.rem(mine + offset + 2 * y_lo, 4)
                column = y_hi * NX + x
                lanes = slice(256 * y_lo, 256 * y_lo + 256)
                qp_ref[column, :, lanes] = ref[y_hi, y_lo, 0:64, :]
                up_ref[column, :, lanes] = ref[y_hi, y_lo, 64:128, :]
                for t in range(4):
                    at = 1024 * y_lo + 256 * t
                    down_ref[column, :, at : at + 256] = ref[y_hi, y_lo, 128 + 16 * t : 144 + 16 * t, :]


def normalized(wide):
    center = jnp.mean(wide, axis=-1, keepdims=True)
    spread = jnp.mean((wide - center) ** 2, axis=-1, keepdims=True)
    return (wide - center) * lax.rsqrt(spread + EPS)


def norm_kernel(mid_ref, left_ref, right_ref, top_ref, bottom_ref, out_ref):
    for half in range(4):
        if half == 0:
            middle = left_ref[...]
        elif half == 3:
            middle = right_ref[...]
        else:
            middle = mid_ref[half - 1]
        wide = jnp.concatenate(
            [top_ref[half].astype(F32), middle.astype(F32), bottom_ref[half].astype(F32)], axis=0
        )
        out_ref[half] = normalized(wide).astype(BF16)


def labels(index, wraps):
    level = lax.rem(index, 4)
    row = lax.rem(index, 144) // 24
    of_level = jnp.where(level == 3, 1, jnp.where(level == 0, 2, 0))
    return of_level + jnp.where(row >= WH // 2, 4 * wraps, 0)


def attend_kernel(
    s_ref, xn_ref, x_ref, own_ref, other_ref, att_ref, h_ref, wq, wp, keys, values, queries, mixed
):
    core = s_ref[1]

    def place(column, carry):
        for ref, parity in ((own_ref, core), (other_ref, 1 - core)):
            j = 2 * column + parity
            wq[pl.ds(pl.multiple_of(48 * j, 16), 48), :] = ref[column, 0:48, :]
            wp[pl.ds(pl.multiple_of(16 * j, 16), 16), :] = ref[column, 48:64, :]
        return carry

    lax.fori_loop(0, 16, place, 0)

    def project(half, carry):
        rows = xn_ref[half]
        keys[half] = dot_nt(rows, wq[512:1024, :]).astype(BF16)
        values[half] = dot_nt(rows, wq[1024:1536, :]).astype(BF16)
        return carry

    lax.fori_loop(0, 4, project, 0)

    def project_queries(half, carry):
        q = dot_nt(xn_ref[half + 1], wq[0:512, :]).astype(BF16).astype(F32) * HD**-0.5
        queries[half] = q.astype(BF16)
        return carry

    lax.fori_loop(0, 2, project_queries, 0)

    head_of = lax.broadcasted_iota(jnp.int32, (4, 1, 256), 2) // HD
    chosen = head_of == lax.broadcasted_iota(jnp.int32, (4, 1, 256), 0)
    chosen16 = chosen.astype(BF16)
    chosen32 = chosen.astype(F32)

    def heads(step, carry):
        side, group = step // 2, lax.rem(step, 2)
        lanes = pl.ds(pl.multiple_of(group * 256, 256), 256)
        for window in range(3):
            start, stop = ((64, 144), (144, 288), (288, 368))[window]
            count = stop - start
            wraps = s_ref[2] if window == 0 else s_ref[3] if window == 2 else 0
            at = slice(144 * window, 144 * window + 144)
            k = jnp.concatenate([keys[2 * side, at, lanes], keys[2 * side + 1, at, lanes]], axis=0)
            v = jnp.concatenate([values[2 * side, at, lanes], values[2 * side + 1, at, lanes]], axis=0)
            q = queries[side, start:stop, lanes]
            spread = (q[None] * chosen16).reshape(4 * count, 256)
            scores = dot_nt(spread, k).reshape(4, count, 288)
            of_query = labels(lax.broadcasted_iota(jnp.int32, (count, 288), 0) + start, wraps)
            of_key = labels(lax.broadcasted_iota(jnp.int32, (count, 288), 1), wraps)
            scores = jnp.where((of_query == of_key)[None], scores, -1000000000.0)
            weights = jnp.exp(scores - jnp.max(scores, axis=-1, keepdims=True))
            total = jnp.sum(weights, axis=-1, keepdims=True)
            weights = (weights * (1.0 / total)).astype(BF16).reshape(4 * count, 288)
            out = jnp.dot(weights, v, preferred_element_type=F32).reshape(4, count, 256)
            out = jnp.sum(out * chosen32, axis=0)
            if window == 0:
                mixed[side, 0:72, lanes] = out[8:80]
            elif window == 1:
                mixed[side, 72:216, lanes] = out
            else:
                mixed[side, 216:288, lanes] = out[0:72]
        return carry

    lax.fori_loop(0, 4, heads, 0)

    for side in range(2):
        attended = x_ref[side].astype(F32) + dot_nt(mixed[side].astype(BF16), wp[...])
        attended = attended.astype(BF16)
        att_ref[side] = attended
        h_ref[side] = normalized(attended.astype(F32)).astype(BF16)


def feed_kernel(s_ref, h_ref, att_ref, up_own, up_other, down_own, down_other, out_ref, wu, wd):
    core = s_ref[1]

    def place(column, carry):
        for up, down, parity in ((up_own, down_own, core), (up_other, down_other, 1 - core)):
            j = 2 * column + parity
            wu[pl.ds(pl.multiple_of(64 * j, 16), 64), :] = up[column]
            wd[pl.ds(pl.multiple_of(16 * j, 16), 16), :] = down[column]
        return carry

    lax.fori_loop(0, 16, place, 0)

    for side in range(2):
        total = att_ref[side].astype(F32)
        for chunk in range(4):
            at = slice(512 * chunk, 512 * chunk + 512)
            hidden = dot_nt(h_ref[side], wu[at, :])
            expanded = 0.5 * hidden * (1.0 + lax.erf(hidden * 0.5**0.5))
            total = total + dot_nt(expanded.astype(BF16), wd[:, at])
        out_ref[side] = total.astype(BF16)


def shift(value, axis, by):
    size = lax.axis_size(axis)
    return lax.ppermute(value, axis, [(i, (i + by) % size) for i in range(size)])


def on_device(tokens, w_qkv, w_proj, w_up, w_down):
    lat, lon = lax.axis_index("lat"), lax.axis_index("lon")
    mine = lax.rem(lax.rem(lon // 2, NX) + 2 * (lat // NZ), 4)
    scalars = jnp.stack(
        [mine, lax.rem(lon, 2), (lat == 0).astype(jnp.int32), (lat == LAT - 1).astype(jnp.int32)]
    ).astype(jnp.int32)

    blob = kernel_call(pack_kernel, jax.ShapeDtypeStruct((LAT, 48, 128), BF16), operands=4)(
        w_qkv, w_proj, w_up, w_down
    )

    mid = tokens.transpose(2, 1, 0, 3).reshape(2, 6, 12, 4, D).transpose(0, 2, 1, 3, 4).reshape(2, 12, 24, D)
    left = shift(mid[1], "lon", 1)
    right = shift(mid[0], "lon", -1)

    gathered = lax.all_to_all(blob, ("lat", "lon"), 0, 0, axis_index_groups=CLASS_GROUPS)
    unit = kernel_call(unit_kernel, jax.ShapeDtypeStruct((2, 192, 256), BF16), operands=1)(gathered)

    last = jnp.stack([left[9:], mid[0, 9:], mid[1, 9:], right[9:]])
    first = jnp.stack([left[:3], mid[0, :3], mid[1, :3], right[:3]])
    top = shift(last, "lat", 1)
    bottom = shift(first, "lat", -1)

    own = lax.all_gather(unit, "lon", axis=0, axis_index_groups=Y_GROUPS)

    def along_x(by):
        return lax.ppermute(
            own,
            "lon",
            [
                (j, 2 * (NX * lon_parts(j)[0] + (lon_parts(j)[1] + by) % NX) + j % 2)
                for j in range(LON)
            ],
        )

    one = along_x(-1)
    three = along_x(1)
    two = lax.ppermute(own, "lat", [(i, i ^ NZ) for i in range(LAT)])

    normed = kernel_call(norm_kernel, jax.ShapeDtypeStruct((4, 432, D), BF16), operands=5)(
        mid.reshape(2, 288, D),
        left.reshape(288, D),
        right.reshape(288, D),
        top.reshape(4, 72, D),
        bottom.reshape(4, 72, D),
    )

    qp, up, down = kernel_call(
        half_kernel,
        (
            jax.ShapeDtypeStruct((16, 64, 512), BF16),
            jax.ShapeDtypeStruct((16, 64, 512), BF16),
            jax.ShapeDtypeStruct((16, 16, 2048), BF16),
        ),
        smem=1,
        operands=4,
    )(scalars, own, one, two, three)
    pairs = [(j, j ^ 1) for j in range(LON)]
    qp_other = lax.ppermute(qp, "lon", pairs)
    up_other = lax.ppermute(up, "lon", pairs)
    down_other = lax.ppermute(down, "lon", pairs)

    attended, h = kernel_call(
        attend_kernel,
        (jax.ShapeDtypeStruct((2, 288, D), BF16), jax.ShapeDtypeStruct((2, 288, D), BF16)),
        scratch=[
            pltpu.VMEM((1536, D), BF16),
            pltpu.VMEM((D, D), BF16),
            pltpu.VMEM((4, 432, D), BF16),
            pltpu.VMEM((4, 432, D), BF16),
            pltpu.VMEM((2, 432, D), BF16),
            pltpu.VMEM((2, 288, D), F32),
        ],
        smem=1,
        operands=4,
        cost=pl.CostEstimate(flops=4_000_000_000, bytes_accessed=8_000_000, transcendentals=1_800_000),
    )(scalars, normed, mid.reshape(2, 288, D), qp, qp_other)

    block = kernel_call(
        feed_kernel,
        jax.ShapeDtypeStruct((2, 288, D), BF16),
        scratch=[pltpu.VMEM((FF, D), BF16), pltpu.VMEM((D, FF), BF16)],
        smem=1,
        operands=6,
        cost=pl.CostEstimate(flops=2_400_000_000, bytes_accessed=8_000_000, transcendentals=1_200_000),
    )(scalars, h, attended, up, up_other, down, down_other)
    return (
        block.reshape(2, 12, 6, 4, D).transpose(3, 1, 0, 2, 4).reshape(4, 12, 12, D)
    )


def solution(mesh):
    weight = P("lat", "lon")
    grid = P(None, "lat", "lon", None)
    return jax.shard_map(
        on_device, mesh=mesh, in_specs=(grid, weight, weight, weight, weight), out_specs=grid, check_vma=False
    )
```

```python
import functools

import jax
import jax.numpy as jnp
from jax import lax
from jax.experimental import pallas as pl
from jax.experimental.pallas import tpu as pltpu
from jax.sharding import PartitionSpec as P

D = 512
FF = 2048
HD = 64
HEADS = 8
WH = 6
EPS = 1e-05
F32 = jnp.float32
BF16 = jnp.bfloat16

NZ, NX = 8, 4
LAT, LON = 16, 32
VMEM_LIMIT = 24 * 1024 * 1024


def place_of(n):
    i, j = n % LAT, n // LAT
    return 2 * (j // (2 * NX)) + i // NZ, (j // 2) % NX, i % NZ, j % 2


def device_at(y, x, z, core):
    y, x, z = y % 8, x % NX, z % NZ
    return NZ * (y % 2) + z + LAT * (2 * (NX * (y // 2) + x) + core)


def class_groups():
    return [
        [device_at(y, kind - 2 * y, z, core) for y in range(8) for z in range(NZ)]
        for core in range(2)
        for kind in range(4)
    ]


def by_chip(value, target):
    return lax.ppermute(
        value, ("lon", "lat"), [(n, device_at(*target(*place_of(n)))) for n in range(LAT * LON)]
    )


def dot_nt(a, b):
    return lax.dot_general(a, b, (((1,), (1,)), ((), ())), preferred_element_type=F32)


def kernel_call(body, out_shape, scratch=(), smem=0, cost=None, keep=True):
    vmem = pl.BlockSpec(memory_space=pltpu.VMEM)

    def call(*args):
        space = pltpu.VMEM if keep else pltpu.HBM
        arrays = [pltpu.with_memory_space_constraint(array, space) for array in args[smem:]]
        return pl.pallas_call(
            body,
            out_shape=out_shape,
            in_specs=[pl.BlockSpec(memory_space=pltpu.SMEM)] * smem + [vmem] * len(arrays),
            out_specs=jax.tree.map(lambda _: vmem, out_shape),
            scratch_shapes=list(scratch),
            compiler_params=pltpu.CompilerParams(vmem_limit_bytes=VMEM_LIMIT),
            cost_estimate=cost,
        )(*args[:smem], *arrays)

    return call


def pack_kernel(qkv_ref, proj_ref, up_ref, down_ref, out_ref):
    rows = jnp.concatenate(
        [qkv_ref[...].astype(F32), proj_ref[...].astype(F32).T, up_ref[...].astype(F32)], axis=1
    )
    blob = jnp.concatenate([rows, down_ref[...].astype(F32)], axis=0).astype(BF16)
    out_ref[...] = jnp.broadcast_to(blob[None], out_ref.shape)


def unit_kernel(in_ref, out_ref):
    for y in range(8):
        for z in range(NZ):
            out_ref[y, 256 + 16 * z : 272 + 16 * z, :] = in_ref[NZ * y + z, 32:48, :]
        for high in range(2):
            first = NZ * y + 4 * high
            rows = jnp.concatenate([in_ref[first + t, 0:32, :] for t in range(4)], axis=0)
            out_ref[y, 128 * high : 128 * high + 128, :] = rows.astype(F32).T.astype(BF16)


def half_kernel(s_ref, own_ref, one_ref, two_ref, three_ref, qp_ref, ff_ref):
    mine = s_ref[0]
    for offset, ref in enumerate((own_ref, one_ref, two_ref, three_ref)):
        for y_hi in range(4):
            for y_lo in range(2):
                x = (mine + offset + 2 * y_lo) & 3
                column = y_hi * NX + x
                unit = 2 * y_hi + y_lo
                for high in range(2):
                    lanes = slice(256 * y_lo + 128 * high, 256 * y_lo + 128 * high + 128)
                    rows = slice(64 + 32 * y_lo + 16 * high, 80 + 32 * y_lo + 16 * high)
                    qp_ref[column, :, lanes] = ref[unit, 128 * high : 128 * high + 64, :]
                    ff_ref[column, 0:64, lanes] = ref[unit, 128 * high + 64 : 128 * high + 128, :]
                    for z in range(4):
                        start = 256 + 16 * (4 * high + z)
                        ff_ref[column, rows, 128 * z : 128 * z + 128] = ref[unit, start : start + 16, :]


def normalized(wide):
    center = jnp.mean(wide, axis=-1, keepdims=True)
    spread = jnp.mean((wide - center) ** 2, axis=-1, keepdims=True)
    return (wide - center) * lax.rsqrt(spread + EPS)


def norm_kernel(mid_ref, left_ref, right_ref, top_ref, bottom_ref, out_ref):
    for half in range(4):
        if half == 0:
            middle = left_ref[...]
        elif half == 3:
            middle = right_ref[...]
        else:
            middle = mid_ref[half - 1]
        wide = jnp.concatenate(
            [top_ref[half].astype(F32), middle.astype(F32), bottom_ref[half].astype(F32)], axis=0
        )
        out_ref[half] = normalized(wide).astype(BF16)


def labels(index, wraps):
    level = lax.rem(index, 4)
    row = lax.rem(index, 144) // 24
    of_level = jnp.where(level == 3, 1, jnp.where(level == 0, 2, 0))
    return of_level + jnp.where(row >= WH // 2, 4 * wraps, 0)


def attend_kernel(
    s_ref, xn_ref, x_ref, own_ref, other_ref, att_ref, h_ref, wq, wp, keys, values, queries, mixed
):
    core = s_ref[1]

    def place(column, carry):
        for ref, parity in ((own_ref, core), (other_ref, 1 - core)):
            j = 2 * column + parity
            wq[pl.ds(pl.multiple_of(48 * j, 16), 48), :] = ref[column, 0:48, :]
            wp[pl.ds(pl.multiple_of(16 * j, 16), 16), :] = ref[column, 48:64, :]
        return carry

    lax.fori_loop(0, 16, place, 0)

    def project(half, carry):
        rows = xn_ref[half]
        keys[half] = dot_nt(rows, wq[512:1024, :]).astype(BF16)
        values[half] = dot_nt(rows, wq[1024:1536, :]).astype(BF16)
        return carry

    lax.fori_loop(0, 4, project, 0)

    def project_queries(half, carry):
        q = dot_nt(xn_ref[half + 1], wq[0:512, :]).astype(BF16).astype(F32) * HD**-0.5
        queries[half] = q.astype(BF16)
        return carry

    lax.fori_loop(0, 2, project_queries, 0)

    head_of = lax.broadcasted_iota(jnp.int32, (4, 1, 256), 2) // HD
    chosen = head_of == lax.broadcasted_iota(jnp.int32, (4, 1, 256), 0)
    chosen16 = chosen.astype(BF16)
    chosen32 = chosen.astype(F32)

    def heads(step, carry):
        side, group = step // 2, lax.rem(step, 2)
        lanes = pl.ds(pl.multiple_of(group * 256, 256), 256)
        for window in range(3):
            start, stop = ((64, 144), (144, 288), (288, 368))[window]
            count = stop - start
            wraps = s_ref[2] if window == 0 else s_ref[3] if window == 2 else 0
            at = slice(144 * window, 144 * window + 144)
            k = jnp.concatenate([keys[2 * side, at, lanes], keys[2 * side + 1, at, lanes]], axis=0)
            v = jnp.concatenate([values[2 * side, at, lanes], values[2 * side + 1, at, lanes]], axis=0)
            q = queries[side, start:stop, lanes]
            spread = (q[None] * chosen16).reshape(4 * count, 256)
            scores = dot_nt(spread, k).reshape(4, count, 288)
            of_query = labels(lax.broadcasted_iota(jnp.int32, (count, 288), 0) + start, wraps)
            of_key = labels(lax.broadcasted_iota(jnp.int32, (count, 288), 1), wraps)
            scores = jnp.where((of_query == of_key)[None], scores, -1000000000.0)
            weights = jnp.exp(scores - jnp.max(scores, axis=-1, keepdims=True))
            total = jnp.sum(weights, axis=-1, keepdims=True)
            weights = (weights * (1.0 / total)).astype(BF16).reshape(4 * count, 288)
            out = jnp.dot(weights, v, preferred_element_type=F32).reshape(4, count, 256)
            out = jnp.sum(out * chosen32, axis=0)
            if window == 0:
                mixed[side, 0:72, lanes] = out[8:80]
            elif window == 1:
                mixed[side, 72:216, lanes] = out
            else:
                mixed[side, 216:288, lanes] = out[0:72]
        return carry

    lax.fori_loop(0, 4, heads, 0)

    for side in range(2):
        attended = x_ref[side].astype(F32) + dot_nt(mixed[side].astype(BF16), wp[...])
        attended = attended.astype(BF16)
        att_ref[side] = attended
        h_ref[side] = normalized(attended.astype(F32)).astype(BF16)


def feed_kernel(s_ref, h_ref, att_ref, own_ref, other_ref, out_ref, wu, wd, wide):
    core = s_ref[1]

    def place(column, carry):
        for ref, parity in ((own_ref, core), (other_ref, 1 - core)):
            j = 2 * column + parity
            wu[pl.ds(pl.multiple_of(64 * j, 16), 64), :] = ref[column, 0:64, :]
            for t in range(4):
                at = slice(64 + 16 * t, 80 + 16 * t)
                wd[pl.ds(pl.multiple_of(16 * j, 16), 16), 512 * t : 512 * t + 512] = ref[column, at, :]
        return carry

    lax.fori_loop(0, 16, place, 0)

    for side in range(2):
        total = att_ref[side].astype(F32)
        for chunk in range(4):
            at = slice(512 * chunk, 512 * chunk + 512)
            hidden = dot_nt(h_ref[side], wu[at, :])
            expanded = 0.5 * hidden * (1.0 + lax.erf(hidden * 0.5**0.5))
            total = total + dot_nt(expanded.astype(BF16), wd[:, at])
        wide[:, 24 * side : 24 * side + 24, :] = total.reshape(12, 24, D)
    out_ref[...] = wide[...].astype(BF16)


def shift(value, axis, by):
    size = lax.axis_size(axis)
    return lax.ppermute(value, axis, [(i, (i + by) % size) for i in range(size)])


def shift_core(value):
    return lax.ppermute(value, "lon", [(j, j ^ 1) for j in range(LON)])


def on_device(tokens, w_qkv, w_proj, w_up, w_down):
    lat, lon = lax.axis_index("lat"), lax.axis_index("lon")
    mine = ((lon >> 1) + 2 * (lat >> 3)) & 3
    scalars = jnp.stack(
        [mine, lon & 1, (lat == 0).astype(jnp.int32), (lat == LAT - 1).astype(jnp.int32)]
    ).astype(jnp.int32)

    blob = kernel_call(pack_kernel, jax.ShapeDtypeStruct((64, 48, 128), BF16), keep=False)(
        w_qkv, w_proj.T, w_up, w_down.T
    )
    gathered = lax.all_to_all(blob, ("lon", "lat"), 0, 0, axis_index_groups=class_groups())

    mid = tokens.transpose(2, 1, 0, 3).reshape(2, 6, 12, 4, D).transpose(0, 2, 1, 3, 4).reshape(2, 12, 24, D)
    left = shift(mid[1], "lon", 1)
    right = shift(mid[0], "lon", -1)

    own = kernel_call(unit_kernel, jax.ShapeDtypeStruct((8, 384, 128), BF16))(gathered)
    own, left, right = lax.optimization_barrier((own, left, right))

    last = jnp.stack([left[9:], mid[0, 9:], mid[1, 9:], right[9:]])
    first = jnp.stack([left[:3], mid[0, :3], mid[1, :3], right[:3]])
    top = shift(last, "lat", 1)
    bottom = shift(first, "lat", -1)

    one = by_chip(own, lambda y, x, z, core: (y, x - 1, z, core))
    three = by_chip(own, lambda y, x, z, core: (y, x + 1, z, core))
    two = by_chip(own, lambda y, x, z, core: (y ^ 1, x, z, core))

    normed = kernel_call(norm_kernel, jax.ShapeDtypeStruct((4, 432, D), BF16))(
        mid.reshape(2, 288, D),
        left.reshape(288, D),
        right.reshape(288, D),
        top.reshape(4, 72, D),
        bottom.reshape(4, 72, D),
    )
    one, normed = lax.optimization_barrier((one, normed))

    qp, ff = kernel_call(
        half_kernel,
        (jax.ShapeDtypeStruct((16, 64, 512), BF16), jax.ShapeDtypeStruct((16, 128, 512), BF16)),
        smem=1,
    )(scalars, own, one, two, three)
    qp_other = shift_core(qp)
    ff_other = shift_core(ff)

    attended, h = kernel_call(
        attend_kernel,
        (jax.ShapeDtypeStruct((2, 288, D), BF16), jax.ShapeDtypeStruct((2, 288, D), BF16)),
        scratch=[
            pltpu.VMEM((1536, D), BF16),
            pltpu.VMEM((D, D), BF16),
            pltpu.VMEM((4, 432, D), BF16),
            pltpu.VMEM((4, 432, D), BF16),
            pltpu.VMEM((2, 432, D), BF16),
            pltpu.VMEM((2, 288, D), F32),
        ],
        smem=1,
        cost=pl.CostEstimate(flops=4_000_000_000, bytes_accessed=8_000_000, transcendentals=1_800_000),
    )(scalars, normed, mid.reshape(2, 288, D), qp, qp_other)

    block = kernel_call(
        feed_kernel,
        jax.ShapeDtypeStruct((12, 48, D), BF16),
        scratch=[
            pltpu.VMEM((FF, D), BF16),
            pltpu.VMEM((D, FF), BF16),
            pltpu.VMEM((12, 48, D), F32),
        ],
        smem=1,
        cost=pl.CostEstimate(flops=2_400_000_000, bytes_accessed=8_000_000, transcendentals=1_200_000),
    )(scalars, h, attended, ff, ff_other)
    return block.reshape(12, 12, 4, D).transpose(2, 0, 1, 3)


def solution(mesh):
    weight = P("lat", "lon")
    grid = P(None, "lat", "lon", None)
    return jax.shard_map(
        on_device, mesh=mesh, in_specs=(grid, weight, weight, weight, weight), out_specs=grid, check_vma=False
    )
```

```python
import functools

import jax
import jax.numpy as jnp
from jax import lax
from jax.experimental import pallas as pl
from jax.experimental.pallas import tpu as pltpu
from jax.sharding import PartitionSpec as P

D = 512
FF = 2048
HD = 64
HEADS = 8
WH = 6
EPS = 1e-05
F32 = jnp.float32
BF16 = jnp.bfloat16

NZ, NX = 8, 4
LAT, LON = 16, 32
VMEM_LIMIT = 24 * 1024 * 1024


def place_of(n):
    i, j = n % LAT, n // LAT
    return 2 * (j // (2 * NX)) + i // NZ, (j // 2) % NX, i % NZ, j % 2


def device_at(y, x, z, core):
    y, x, z = y % 8, x % NX, z % NZ
    return NZ * (y % 2) + z + LAT * (2 * (NX * (y // 2) + x) + core)


def class_groups():
    return [
        [device_at(y, kind - 2 * y, z, core) for y in range(8) for z in range(NZ)]
        for core in range(2)
        for kind in range(4)
    ]


def by_chip(value, target):
    return lax.ppermute(
        value, ("lon", "lat"), [(n, device_at(*target(*place_of(n)))) for n in range(LAT * LON)]
    )


def dot_nt(a, b):
    return lax.dot_general(a, b, (((1,), (1,)), ((), ())), preferred_element_type=F32)


def kernel_call(body, out_shape, scratch=(), smem=0, cost=None, keep=True):
    vmem = pl.BlockSpec(memory_space=pltpu.VMEM)

    def call(*args):
        space = pltpu.VMEM if keep else pltpu.HBM
        arrays = [pltpu.with_memory_space_constraint(array, space) for array in args[smem:]]
        return pl.pallas_call(
            body,
            out_shape=jax.tree.map(lambda out: pltpu.VMEM(out.shape, out.dtype), out_shape),
            in_specs=[pl.BlockSpec(memory_space=pltpu.SMEM)] * smem + [vmem] * len(arrays),
            out_specs=jax.tree.map(lambda _: vmem, out_shape),
            scratch_shapes=list(scratch),
            compiler_params=pltpu.CompilerParams(vmem_limit_bytes=VMEM_LIMIT),
            cost_estimate=cost,
        )(*args[:smem], *arrays)

    return call


def pack_kernel(qkv_ref, proj_ref, up_ref, down_ref, out_ref):
    rows = jnp.concatenate(
        [qkv_ref[...].astype(F32), proj_ref[...].astype(F32).T, up_ref[...].astype(F32)], axis=1
    )
    blob = jnp.concatenate([rows, down_ref[...].astype(F32)], axis=0).astype(BF16)
    out_ref[...] = jnp.broadcast_to(blob[None], out_ref.shape)


def unit_kernel(in_ref, out_ref):
    for y in range(8):
        for z in range(NZ):
            out_ref[y, 256 + 16 * z : 272 + 16 * z, :] = in_ref[NZ * y + z, 32:48, :]
        for high in range(2):
            first = NZ * y + 4 * high
            rows = jnp.concatenate([in_ref[first + t, 0:32, :] for t in range(4)], axis=0)
            out_ref[y, 128 * high : 128 * high + 128, :] = rows.astype(F32).T.astype(BF16)


def columns(mine):
    for offset in range(4):
        for y in range(8):
            yield offset, y, (y // 2) * NX + ((mine + offset + 2 * y) & 3)


def half_qp_kernel(s_ref, own_ref, one_ref, two_ref, three_ref, qp_ref):
    refs = (own_ref, one_ref, two_ref, three_ref)
    for offset, y, column in columns(s_ref[0]):
        for high in range(2):
            at = 256 * (y % 2) + 128 * high
            qp_ref[column, :, at : at + 128] = refs[offset][y, 128 * high : 128 * high + 64, :]


def half_ff_kernel(s_ref, own_ref, one_ref, two_ref, three_ref, ff_ref):
    refs = (own_ref, one_ref, two_ref, three_ref)
    for offset, y, column in columns(s_ref[0]):
        ref = refs[offset]
        for high in range(2):
            at = 256 * (y % 2) + 128 * high
            ff_ref[column, 0:64, at : at + 128] = ref[y, 128 * high + 64 : 128 * high + 128, :]
            rows = slice(64 + 32 * (y % 2) + 16 * high, 80 + 32 * (y % 2) + 16 * high)
            for z in range(4):
                start = 256 + 16 * (4 * high + z)
                ff_ref[column, rows, 128 * z : 128 * z + 128] = ref[y, start : start + 16, :]


def normalized(wide):
    center = jnp.mean(wide, axis=-1, keepdims=True)
    spread = jnp.mean((wide - center) ** 2, axis=-1, keepdims=True)
    return (wide - center) * lax.rsqrt(spread + EPS)


def norm_kernel(mid_ref, left_ref, right_ref, top_ref, bottom_ref, out_ref):
    for half in range(4):
        if half == 0:
            middle = left_ref[...]
        elif half == 3:
            middle = right_ref[...]
        else:
            middle = mid_ref[half - 1]
        wide = jnp.concatenate(
            [top_ref[half].astype(F32), middle.astype(F32), bottom_ref[half].astype(F32)], axis=0
        )
        out_ref[half] = normalized(wide).astype(BF16)


def edge_kernel(mid_ref, left_ref, right_ref, first_ref, last_ref):
    for half in range(4):
        ref = left_ref if half == 0 else right_ref if half == 3 else mid_ref.at[half - 1]
        first_ref[half] = ref[0:3]
        last_ref[half] = ref[9:12]


def labels(index, wraps):
    level = lax.rem(index, 4)
    row = lax.rem(index, 144) // 24
    of_level = jnp.where(level == 3, 1, jnp.where(level == 0, 2, 0))
    return of_level + jnp.where(row >= WH // 2, 4 * wraps, 0)


def attend_kernel(
    s_ref, xn_ref, x_ref, own_ref, other_ref, att_ref, h_ref, wq, wp, keys, values, queries, mixed
):
    core = s_ref[1]

    def place(column, carry):
        for ref, parity in ((own_ref, core), (other_ref, 1 - core)):
            j = 2 * column + parity
            wq[pl.ds(pl.multiple_of(48 * j, 16), 48), :] = ref[column, 0:48, :]
            wp[pl.ds(pl.multiple_of(16 * j, 16), 16), :] = ref[column, 48:64, :]
        return carry

    lax.fori_loop(0, 16, place, 0)

    for half in range(4):
        rows = xn_ref[half]
        keys[half] = dot_nt(rows, wq[512:1024, :]).astype(BF16)
        values[half] = dot_nt(rows, wq[1024:1536, :]).astype(BF16)

    for half in range(2):
        q = dot_nt(xn_ref[half + 1], wq[0:512, :]).astype(BF16).astype(F32) * HD**-0.5
        queries[half] = q.astype(BF16)

    head_of = lax.broadcasted_iota(jnp.int32, (4, 1, 256), 2) // HD
    chosen = head_of == lax.broadcasted_iota(jnp.int32, (4, 1, 256), 0)
    chosen16 = chosen.astype(BF16)
    chosen32 = chosen.astype(F32)

    def heads(side, group):
        lanes = slice(group * 256, group * 256 + 256)
        for window in range(3):
            start, stop = ((64, 144), (144, 288), (288, 368))[window]
            count = stop - start
            wraps = s_ref[2] if window == 0 else s_ref[3] if window == 2 else 0
            at = slice(144 * window, 144 * window + 144)
            k = jnp.concatenate([keys[2 * side, at, lanes], keys[2 * side + 1, at, lanes]], axis=0)
            v = jnp.concatenate([values[2 * side, at, lanes], values[2 * side + 1, at, lanes]], axis=0)
            q = queries[side, start:stop, lanes]
            spread = (q[None] * chosen16).reshape(4 * count, 256)
            scores = dot_nt(spread, k).reshape(4, count, 288)
            of_query = labels(lax.broadcasted_iota(jnp.int32, (count, 288), 0) + start, wraps)
            of_key = labels(lax.broadcasted_iota(jnp.int32, (count, 288), 1), wraps)
            scores = jnp.where((of_query == of_key)[None], scores, -1000000000.0)
            weights = jnp.exp(scores - jnp.max(scores, axis=-1, keepdims=True))
            total = jnp.sum(weights, axis=-1, keepdims=True)
            weights = weights.astype(BF16).reshape(4 * count, 288)
            out = jnp.dot(weights, v, preferred_element_type=F32).reshape(4, count, 256)
            out = jnp.sum(out * (chosen32 * (1.0 / total)), axis=0)
            if window == 0:
                mixed[side, 0:72, lanes] = out[8:80]
            elif window == 1:
                mixed[side, 72:216, lanes] = out
            else:
                mixed[side, 216:288, lanes] = out[0:72]

    for step in range(4):
        heads(step // 2, step % 2)

    for side in range(2):
        attended = x_ref[side].astype(F32) + dot_nt(mixed[side].astype(BF16), wp[...])
        attended = attended.astype(BF16)
        att_ref[side] = attended
        h_ref[side] = normalized(attended.astype(F32)).astype(BF16)


def feed_kernel(s_ref, h_ref, att_ref, own_ref, other_ref, out_ref, wu, wd, wide):
    core = s_ref[1]

    def place(column, carry):
        for ref, parity in ((own_ref, core), (other_ref, 1 - core)):
            j = 2 * column + parity
            wu[pl.ds(pl.multiple_of(64 * j, 16), 64), :] = ref[column, 0:64, :]
            for t in range(4):
                at = slice(64 + 16 * t, 80 + 16 * t)
                wd[pl.ds(pl.multiple_of(16 * j, 16), 16), 512 * t : 512 * t + 512] = ref[column, at, :]
        return carry

    lax.fori_loop(0, 16, place, 0)

    for side in range(2):
        total = att_ref[side].astype(F32)
        for chunk in range(2):
            at = slice(1024 * chunk, 1024 * chunk + 1024)
            hidden = dot_nt(h_ref[side], wu[at, :])
            expanded = 0.5 * hidden * (1.0 + lax.erf(hidden * 0.5**0.5))
            total = total + dot_nt(expanded.astype(BF16), wd[:, at])
        wide[:, 24 * side : 24 * side + 24, :] = total.reshape(12, 24, D)
    out_ref[...] = wide[...].astype(BF16)


def shift(value, axis, by):
    size = lax.axis_size(axis)
    return lax.ppermute(value, axis, [(i, (i + by) % size) for i in range(size)])


def shift_core(value):
    return lax.ppermute(value, "lon", [(j, j ^ 1) for j in range(LON)])


def on_device(tokens, w_qkv, w_proj, w_up, w_down):
    lat, lon = lax.axis_index("lat"), lax.axis_index("lon")
    mine = ((lon >> 1) + 2 * (lat >> 3)) & 3
    scalars = jnp.stack(
        [mine, lon & 1, (lat == 0).astype(jnp.int32), (lat == LAT - 1).astype(jnp.int32)]
    ).astype(jnp.int32)

    blob = kernel_call(pack_kernel, jax.ShapeDtypeStruct((64, 48, 128), BF16), keep=False)(
        w_qkv, w_proj.T, w_up, w_down.T
    )
    gathered = lax.all_to_all(blob, ("lon", "lat"), 0, 0, axis_index_groups=class_groups())

    mid = tokens.transpose(2, 1, 0, 3).reshape(2, 6, 12, 4, D).transpose(0, 2, 1, 3, 4).reshape(2, 12, 24, D)
    mid = lax.optimization_barrier(mid)
    left = shift(mid[1], "lon", 1)
    right = shift(mid[0], "lon", -1)

    own = kernel_call(unit_kernel, jax.ShapeDtypeStruct((8, 384, 128), BF16))(gathered)
    own, left, right = lax.optimization_barrier((own, left, right))
    weights = (
        own,
        by_chip(own, lambda y, x, z, core: (y, x - 1, z, core)),
        by_chip(own, lambda y, x, z, core: (y ^ 1, x, z, core)),
        by_chip(own, lambda y, x, z, core: (y, x + 1, z, core)),
    )

    edge = jax.ShapeDtypeStruct((4, 3, 24, D), BF16)
    first, last = kernel_call(edge_kernel, (edge, edge))(mid, left, right)
    top = shift(last, "lat", 1)
    bottom = shift(first, "lat", -1)

    weights, top, bottom = lax.optimization_barrier((weights, top, bottom))
    qp = kernel_call(half_qp_kernel, jax.ShapeDtypeStruct((16, 64, 512), BF16), smem=1)(scalars, *weights)
    qp_other = shift_core(qp)
    ff = kernel_call(half_ff_kernel, jax.ShapeDtypeStruct((16, 128, 512), BF16), smem=1)(scalars, *weights)
    ff_other = shift_core(ff)

    normed = kernel_call(norm_kernel, jax.ShapeDtypeStruct((4, 432, D), BF16))(
        mid.reshape(2, 288, D),
        left.reshape(288, D),
        right.reshape(288, D),
        top.reshape(4, 72, D),
        bottom.reshape(4, 72, D),
    )

    attended, h = kernel_call(
        attend_kernel,
        (jax.ShapeDtypeStruct((2, 288, D), BF16), jax.ShapeDtypeStruct((2, 288, D), BF16)),
        scratch=[
            pltpu.VMEM((1536, D), BF16),
            pltpu.VMEM((D, D), BF16),
            pltpu.VMEM((4, 432, D), BF16),
            pltpu.VMEM((4, 432, D), BF16),
            pltpu.VMEM((2, 432, D), BF16),
            pltpu.VMEM((2, 288, D), F32),
        ],
        smem=1,
        cost=pl.CostEstimate(flops=4_000_000_000, bytes_accessed=8_000_000, transcendentals=1_800_000),
    )(scalars, normed, mid.reshape(2, 288, D), qp, qp_other)

    block = kernel_call(
        feed_kernel,
        jax.ShapeDtypeStruct((12, 48, D), BF16),
        scratch=[
            pltpu.VMEM((FF, D), BF16),
            pltpu.VMEM((D, FF), BF16),
            pltpu.VMEM((12, 48, D), F32),
        ],
        smem=1,
        cost=pl.CostEstimate(flops=2_400_000_000, bytes_accessed=8_000_000, transcendentals=1_200_000),
    )(scalars, h, attended, ff, ff_other)
    return block.reshape(12, 12, 4, D).transpose(2, 0, 1, 3)


def solution(mesh):
    weight = P("lat", "lon")
    grid = P(None, "lat", "lon", None)
    return jax.shard_map(
        on_device, mesh=mesh, in_specs=(grid, weight, weight, weight, weight), out_specs=grid, check_vma=False
    )
```

```python
import functools

import jax
import jax.numpy as jnp
from jax import lax
from jax.experimental import pallas as pl
from jax.experimental.pallas import tpu as pltpu
from jax.sharding import PartitionSpec as P

D = 512
FF = 2048
HD = 64
HEADS = 8
WH = 6
EPS = 1e-05
F32 = jnp.float32
BF16 = jnp.bfloat16

NZ, NX = 8, 4
LAT, LON = 16, 32
VMEM_LIMIT = 24 * 1024 * 1024


def place_of(n):
    i, j = n % LAT, n // LAT
    return 2 * (j // (2 * NX)) + i // NZ, (j // 2) % NX, i % NZ, j % 2


def device_at(y, x, z, core):
    y, x, z = y % 8, x % NX, z % NZ
    return NZ * (y % 2) + z + LAT * (2 * (NX * (y // 2) + x) + core)


def class_groups():
    return [
        [device_at(y, kind - 2 * y, z, core) for y in range(8) for z in range(NZ)]
        for core in range(2)
        for kind in range(4)
    ]


def by_chip(value, target):
    return lax.ppermute(
        value, ("lon", "lat"), [(n, device_at(*target(*place_of(n)))) for n in range(LAT * LON)]
    )


def dot_nt(a, b):
    return lax.dot_general(a, b, (((1,), (1,)), ((), ())), preferred_element_type=F32)


def kernel_call(body, out_shape, scratch=(), smem=0, cost=None, keep=True):
    vmem = pl.BlockSpec(memory_space=pltpu.VMEM)

    def call(*args):
        space = pltpu.VMEM if keep else pltpu.HBM
        arrays = [pltpu.with_memory_space_constraint(array, space) for array in args[smem:]]
        return pl.pallas_call(
            body,
            out_shape=jax.tree.map(lambda out: pltpu.VMEM(out.shape, out.dtype), out_shape),
            in_specs=[pl.BlockSpec(memory_space=pltpu.SMEM)] * smem + [vmem] * len(arrays),
            out_specs=jax.tree.map(lambda _: vmem, out_shape),
            scratch_shapes=list(scratch),
            compiler_params=pltpu.CompilerParams(vmem_limit_bytes=VMEM_LIMIT),
            cost_estimate=cost,
        )(*args[:smem], *arrays)

    return call


def pack_kernel(qkv_ref, proj_ref, up_ref, down_ref, out_ref):
    rows = jnp.concatenate(
        [qkv_ref[...].astype(F32), proj_ref[...].astype(F32).T, up_ref[...].astype(F32)], axis=1
    )
    blob = jnp.concatenate([rows, down_ref[...].astype(F32)], axis=0).astype(BF16)
    out_ref[...] = jnp.broadcast_to(blob[None], out_ref.shape)


def unit_kernel(in_ref, out_ref):
    for y in range(8):
        for z in range(NZ):
            out_ref[y, 256 + 16 * z : 272 + 16 * z, :] = in_ref[NZ * y + z, 32:48, :]
        for high in range(2):
            first = NZ * y + 4 * high
            rows = jnp.concatenate([in_ref[first + t, 0:32, :] for t in range(4)], axis=0)
            out_ref[y, 128 * high : 128 * high + 128, :] = rows.astype(F32).T.astype(BF16)


def columns(mine):
    for offset in range(4):
        for y in range(8):
            yield offset, y, (y // 2) * NX + ((mine + offset + 2 * y) & 3)


def half_qp_kernel(s_ref, own_ref, one_ref, two_ref, three_ref, qp_ref):
    refs = (own_ref, one_ref, two_ref, three_ref)
    for offset, y, column in columns(s_ref[0]):
        for high in range(2):
            at = 256 * (y % 2) + 128 * high
            qp_ref[column, :, at : at + 128] = refs[offset][y, 128 * high : 128 * high + 64, :]


def half_ff_kernel(s_ref, own_ref, one_ref, two_ref, three_ref, ff_ref):
    refs = (own_ref, one_ref, two_ref, three_ref)
    for offset, y, column in columns(s_ref[0]):
        ref = refs[offset]
        for high in range(2):
            at = 256 * (y % 2) + 128 * high
            ff_ref[column, 0:64, at : at + 128] = ref[y, 128 * high + 64 : 128 * high + 128, :]
            rows = slice(64 + 32 * (y % 2) + 16 * high, 80 + 32 * (y % 2) + 16 * high)
            for z in range(4):
                start = 256 + 16 * (4 * high + z)
                ff_ref[column, rows, 128 * z : 128 * z + 128] = ref[y, start : start + 16, :]


def normalized(wide):
    center = jnp.mean(wide, axis=-1, keepdims=True)
    spread = jnp.mean((wide - center) ** 2, axis=-1, keepdims=True)
    return (wide - center) * lax.rsqrt(spread + EPS)


def norm_kernel(mid_ref, left_ref, right_ref, top_ref, bottom_ref, out_ref):
    for half in range(4):
        if half == 0:
            middle = left_ref[...]
        elif half == 3:
            middle = right_ref[...]
        else:
            middle = mid_ref[half - 1]
        wide = jnp.concatenate(
            [top_ref[half].astype(F32), middle.astype(F32), bottom_ref[half].astype(F32)], axis=0
        )
        out_ref[half] = normalized(wide).astype(BF16)


def edge_kernel(mid_ref, left_ref, right_ref, first_ref, last_ref):
    for half in range(4):
        ref = left_ref if half == 0 else right_ref if half == 3 else mid_ref.at[half - 1]
        first_ref[half] = ref[0:3]
        last_ref[half] = ref[9:12]


def labels(index, wraps):
    level = lax.rem(index, 4)
    row = lax.rem(index, 144) // 24
    of_level = jnp.where(level == 3, 1, jnp.where(level == 0, 2, 0))
    return of_level + jnp.where(row >= WH // 2, 4 * wraps, 0)


def attend_kernel(
    s_ref, xn_ref, x_ref, own_ref, other_ref, att_ref, h_ref, wq, wp, keys, values, queries, mixed
):
    core = s_ref[1]

    def place(column, carry):
        for ref, parity in ((own_ref, core), (other_ref, 1 - core)):
            j = 2 * column + parity
            wq[pl.ds(pl.multiple_of(48 * j, 16), 48), :] = ref[column, 0:48, :]
            wp[pl.ds(pl.multiple_of(16 * j, 16), 16), :] = ref[column, 48:64, :]
        return carry

    lax.fori_loop(0, 16, place, 0)

    for half in range(4):
        rows = xn_ref[half]
        keys[half] = dot_nt(rows, wq[512:1024, :]).astype(BF16)
        values[half] = dot_nt(rows, wq[1024:1536, :]).astype(BF16)

    for half in range(2):
        q = dot_nt(xn_ref[half + 1], wq[0:512, :]).astype(BF16).astype(F32) * HD**-0.5
        queries[half] = q.astype(BF16)

    head_of = lax.broadcasted_iota(jnp.int32, (4, 1, 256), 2) // HD
    chosen = head_of == lax.broadcasted_iota(jnp.int32, (4, 1, 256), 0)
    chosen16 = chosen.astype(BF16)
    chosen32 = chosen.astype(F32)

    def heads(side, group):
        lanes = slice(group * 256, group * 256 + 256)
        for window in range(3):
            start, stop = ((64, 144), (144, 288), (288, 368))[window]
            count = stop - start
            wraps = s_ref[2] if window == 0 else s_ref[3] if window == 2 else 0
            at = slice(144 * window, 144 * window + 144)
            k = jnp.concatenate([keys[2 * side, at, lanes], keys[2 * side + 1, at, lanes]], axis=0)
            v = jnp.concatenate([values[2 * side, at, lanes], values[2 * side + 1, at, lanes]], axis=0)
            q = queries[side, start:stop, lanes]
            spread = (q[None] * chosen16).reshape(4 * count, 256)
            scores = dot_nt(spread, k).reshape(4, count, 288)
            of_query = labels(lax.broadcasted_iota(jnp.int32, (count, 288), 0) + start, wraps)
            of_key = labels(lax.broadcasted_iota(jnp.int32, (count, 288), 1), wraps)
            scores = jnp.where((of_query == of_key)[None], scores, -1000000000.0)
            weights = jnp.exp(scores - jnp.max(scores, axis=-1, keepdims=True))
            total = jnp.sum(weights, axis=-1, keepdims=True)
            weights = weights.astype(BF16).reshape(4 * count, 288)
            out = jnp.dot(weights, v, preferred_element_type=F32).reshape(4, count, 256)
            out = jnp.sum(out * (chosen32 * (1.0 / total)), axis=0)
            if window == 0:
                mixed[side, 0:72, lanes] = out[8:80]
            elif window == 1:
                mixed[side, 72:216, lanes] = out
            else:
                mixed[side, 216:288, lanes] = out[0:72]

    for step in range(4):
        heads(step // 2, step % 2)

    for side in range(2):
        attended = x_ref[side].astype(F32) + dot_nt(mixed[side].astype(BF16), wp[...])
        attended = attended.astype(BF16)
        att_ref[side] = attended
        h_ref[side] = normalized(attended.astype(F32)).astype(BF16)


def feed_kernel(s_ref, h_ref, att_ref, own_ref, other_ref, out_ref, wu, wd):
    core = s_ref[1]

    def place(column, carry):
        for ref, parity in ((own_ref, core), (other_ref, 1 - core)):
            j = 2 * column + parity
            wu[pl.ds(pl.multiple_of(64 * j, 16), 64), :] = ref[column, 0:64, :]
            for t in range(4):
                at = slice(64 + 16 * t, 80 + 16 * t)
                wd[pl.ds(pl.multiple_of(16 * j, 16), 16), 512 * t : 512 * t + 512] = ref[column, at, :]
        return carry

    lax.fori_loop(0, 16, place, 0)

    for side in range(2):
        total = att_ref[side].astype(F32)
        for chunk in range(2):
            at = slice(1024 * chunk, 1024 * chunk + 1024)
            hidden = dot_nt(h_ref[side], wu[at, :])
            expanded = 0.5 * hidden * (1.0 + lax.erf(hidden * 0.5**0.5))
            total = total + dot_nt(expanded.astype(BF16), wd[:, at])
        out_ref[:, 6 * side : 6 * side + 6] = total.reshape(12, 6, 4, D).astype(BF16)


def shift(value, axis, by):
    size = lax.axis_size(axis)
    return lax.ppermute(value, axis, [(i, (i + by) % size) for i in range(size)])


def shift_core(value):
    return lax.ppermute(value, "lon", [(j, j ^ 1) for j in range(LON)])


def on_device(tokens, w_qkv, w_proj, w_up, w_down):
    lat, lon = lax.axis_index("lat"), lax.axis_index("lon")
    mine = ((lon >> 1) + 2 * (lat >> 3)) & 3
    scalars = jnp.stack(
        [mine, lon & 1, (lat == 0).astype(jnp.int32), (lat == LAT - 1).astype(jnp.int32)]
    ).astype(jnp.int32)

    blob = kernel_call(pack_kernel, jax.ShapeDtypeStruct((64, 48, 128), BF16), keep=False)(
        w_qkv, w_proj.T, w_up, w_down.T
    )
    gathered = lax.all_to_all(blob, ("lon", "lat"), 0, 0, axis_index_groups=class_groups())

    mid = tokens.transpose(2, 1, 0, 3).reshape(2, 6, 12, 4, D).transpose(0, 2, 1, 3, 4).reshape(2, 12, 24, D)
    mid = lax.optimization_barrier(mid)
    left = shift(mid[1], "lon", 1)
    right = shift(mid[0], "lon", -1)

    own = kernel_call(unit_kernel, jax.ShapeDtypeStruct((8, 384, 128), BF16))(gathered)
    own, left, right = lax.optimization_barrier((own, left, right))
    weights = (
        own,
        by_chip(own, lambda y, x, z, core: (y, x - 1, z, core)),
        by_chip(own, lambda y, x, z, core: (y ^ 1, x, z, core)),
        by_chip(own, lambda y, x, z, core: (y, x + 1, z, core)),
    )

    edge = jax.ShapeDtypeStruct((4, 3, 24, D), BF16)
    first, last = kernel_call(edge_kernel, (edge, edge))(mid, left, right)
    top = shift(last, "lat", 1)
    bottom = shift(first, "lat", -1)

    weights, top, bottom = lax.optimization_barrier((weights, top, bottom))
    qp = kernel_call(half_qp_kernel, jax.ShapeDtypeStruct((16, 64, 512), BF16), smem=1)(scalars, *weights)
    qp_other = shift_core(qp)
    ff = kernel_call(half_ff_kernel, jax.ShapeDtypeStruct((16, 128, 512), BF16), smem=1)(scalars, *weights)
    ff_other = shift_core(ff)

    normed = kernel_call(norm_kernel, jax.ShapeDtypeStruct((4, 432, D), BF16))(
        mid.reshape(2, 288, D),
        left.reshape(288, D),
        right.reshape(288, D),
        top.reshape(4, 72, D),
        bottom.reshape(4, 72, D),
    )

    attended, h = kernel_call(
        attend_kernel,
        (jax.ShapeDtypeStruct((2, 288, D), BF16), jax.ShapeDtypeStruct((2, 288, D), BF16)),
        scratch=[
            pltpu.VMEM((1536, D), BF16),
            pltpu.VMEM((D, D), BF16),
            pltpu.VMEM((4, 432, D), BF16),
            pltpu.VMEM((4, 432, D), BF16),
            pltpu.VMEM((2, 432, D), BF16),
            pltpu.VMEM((2, 288, D), F32),
        ],
        smem=1,
        cost=pl.CostEstimate(flops=4_000_000_000, bytes_accessed=8_000_000, transcendentals=1_800_000),
    )(scalars, normed, mid.reshape(2, 288, D), qp, qp_other)

    block = kernel_call(
        feed_kernel,
        jax.ShapeDtypeStruct((12, 12, 4, D), BF16),
        scratch=[
            pltpu.VMEM((FF, D), BF16),
            pltpu.VMEM((D, FF), BF16),
        ],
        smem=1,
        cost=pl.CostEstimate(flops=2_400_000_000, bytes_accessed=8_000_000, transcendentals=1_200_000),
    )(scalars, h, attended, ff, ff_other)
    return block.transpose(2, 0, 1, 3)


def solution(mesh):
    weight = P("lat", "lon")
    grid = P(None, "lat", "lon", None)
    return jax.shard_map(
        on_device, mesh=mesh, in_specs=(grid, weight, weight, weight, weight), out_specs=grid, check_vma=False
    )
```
